32 devices in a mesh: groups: 2 (over y), docs: 8 (over z, x), help: 2 (over core).
Axes of the slice: x: 2, y: 2, z: 4, core: 2. Of those that a mesh axis runs over, the one named last changes fastest.
Arguments:
- token_states: bfloat16 [4096, 2, 1024], P(('groups', 'docs', 'help')), parts along dimension 0, may hold values from -6 to 6
- lengths: int32 [4096], P(('groups', 'docs', 'help')), parts along dimension 0, may hold values from 1 to 2
- cluster_id: int32 [4096], P(('groups', 'docs', 'help')), parts along dimension 0, may hold values from 0 to 7, as said below
- proj_weight: bfloat16 [1024, 1024], replicated, may hold values from -0.1875 to 0.1875
- proj_bias: float32 [1024], replicated, may hold values from -4 to 4
Outputs:
- max_sim: float32 [4096], P(('groups', 'docs', 'help')), parts along dimension 0
The draws below stay inside these ranges and needn't reach their ends.
There are 2 independent parts, one for each index of `groups`. The reference program is written for one: setup_inputs(seed, part) draws one part's arguments, and reference() takes and returns one part's arrays. A program takes and returns all parts, laid end to end along the dimension named above; an argument that names none is the same for every part. Nothing has to cross between parts.
Inputs may be any that keep to these rules, and one draw needn't show every extreme that they name: `cluster_id`: clusters 1 * k to 1 * k + 1 - 1 form owner k. Among the 128 documents of one device (aligned blocks of the document dimension), at most 32 belong to one owner, and in every draw one owner gets exactly 32 documents from every device.
All inputs are finite; a program needn't handle non-finite values.
Results may differ from the reference program's by a relative error of at most 0.0003.
Values may be sent and summed in bfloat16 or wider, within the bound.
No kernel may reach another device: no remote copies, remote signals or barrier semaphores. Data moves between devices by JAX's collectives and lax.ppermute only.
A program may use at most 64 MiB of HBM per device.

```python
import jax
import jax.numpy as jnp
from jax import lax

D = 1024
SEQ = 2
DOC_DEV = 128
CL_OWN = 1
CAP = 32
DOCS = 2048
CLUSTERS = 8


def draw_cluster_id(key, part):
    blocks = DOCS // DOC_DEV
    owners = CLUSTERS // CL_OWN
    position_count = owners * CAP
    key_hot, key_pop, key_score, key_order, key_local = jax.random.split(key, 5)
    busiest_holder = jax.random.randint(key_hot, (), 0, owners)
    frequent_clusters = jax.random.randint(key_pop, (owners,), 0, 4)
    position_holder = jnp.arange(position_count, dtype=jnp.int32) // CAP
    extra_reward = frequent_clusters[position_holder] + jnp.where(position_holder == busiest_holder, 8, 0)
    random_jitter = jax.random.randint(key_score, (blocks, position_count), 0, 65536)
    duplicate_scores = (extra_reward[None, :] * 16384 + random_jitter) * position_count + jnp.arange(position_count, dtype=jnp.int32)[None, :]
    top_vals, chosen = lax.top_k(duplicate_scores, DOC_DEV)
    owner_rows = chosen // CAP
    shuffle_keys = jax.random.randint(key_order, (blocks, DOC_DEV), 0, 65536) * DOC_DEV + jnp.arange(DOC_DEV, dtype=jnp.int32)[None, :]
    shuffled_order = jnp.argsort(shuffle_keys, axis=1)
    owner_rows = jnp.take_along_axis(owner_rows, shuffled_order, axis=1).reshape(DOCS)
    local_idx = jax.random.randint(key_local, (DOCS,), 0, CL_OWN)
    return (owner_rows * CL_OWN + local_idx).astype(jnp.int32)


def with_ends(array, stream_key, least, top_value):
    longest = array.shape.index(max(array.shape))
    spots = []
    for shift in (0, 1):
        where = [jax.random.randint(jax.random.fold_in(stream_key, axis), (), 0, length) for axis, length in enumerate(array.shape)]
        where[longest] = (where[longest] + shift) % array.shape[longest]
        spots.append(tuple(where))
    return array.at[spots[0]].set(least).at[spots[1]].set(top_value)


def block_scale(rng, dims, cuts, low, largest):
    gain = 1.0
    for axis_at, blocks in cuts:
        heights = jax.random.uniform(jax.random.fold_in(jax.random.fold_in(rng, 6), axis_at), (blocks,), jnp.float32, low / len(cuts), largest / len(cuts))
        gain = gain * jnp.repeat(jnp.exp(heights), dims[axis_at] // blocks).reshape((-1,) + (1,) * (len(dims) - 1 - axis_at))
    return gain


def centred(own_key, dims, width, most, cuts=(), kind=jnp.bfloat16):
    entries = width * jax.random.normal(own_key, dims, jnp.float32)
    if cuts:
        entries = entries * block_scale(own_key, dims, cuts, -0.22, 0.18)
    return jnp.clip(entries, -most, most).astype(kind)


def setup_inputs(seed: int = 0, part: int = 0) -> dict:
    arg_keys = jax.random.split(jax.random.key(seed), 6)
    part_splits = jax.random.split(jax.random.fold_in(arg_keys[5], part), 6)
    return {
        "token_states": centred(part_splits[0], (DOCS, SEQ, D), 1.0, 6.0, ((0, 16),)),
        "lengths": with_ends(jax.random.randint(part_splits[1], (DOCS,), 1, SEQ + 1), jax.random.fold_in(part_splits[1], 1), 1, SEQ).astype(jnp.int32),
        "cluster_id": draw_cluster_id(jax.random.fold_in(jax.random.fold_in(arg_keys[5], part), 71), part),
        "proj_weight": centred(arg_keys[3], (D, D), D ** -0.5, 0.1875),
        "proj_bias": centred(arg_keys[4], (D,), 1.0, 4.0, (), jnp.float32),
    }


def embed_docs(token_states, lengths, proj_weight, proj_bias):
    seq_len = token_states.shape[1]
    feat_dim = token_states.shape[2]

    def embed_block(pieces):
        states, counts = pieces
        token_mask = (jnp.arange(seq_len, dtype=jnp.int32)[None, :] < counts[:, None]).astype(jnp.float32)
        summed = jnp.einsum('rsd,rs->rd', states.astype(jnp.float32), token_mask)
        pooled = (summed / counts[:, None].astype(jnp.float32)).astype(jnp.bfloat16)
        hidden = jnp.tanh(jnp.dot(pooled, proj_weight, preferred_element_type=jnp.float32) + proj_bias)
        factor = lax.rsqrt(lax.optimization_barrier(jnp.sum(hidden * hidden, axis=1, keepdims=True)) + 1e-06)
        return (hidden * factor).astype(jnp.bfloat16)
    block_count = token_states.shape[0] // DOC_DEV
    shaped = token_states.reshape(block_count, DOC_DEV, seq_len, feat_dim)
    counts = lengths.reshape(block_count, DOC_DEV)
    return lax.map(embed_block, (shaped, counts)).reshape(token_states.shape[0], feat_dim)

def reference(token_states, lengths, cluster_id, proj_weight, proj_bias):
    embedded = embed_docs(token_states, lengths, proj_weight, proj_bias)
    total = cluster_id.shape[0]
    feat_dim = embedded.shape[1]
    sort_order = jnp.argsort(cluster_id, stable=True).astype(jnp.int32)
    sorted_ids = cluster_id[sort_order]
    sorted_emb = embedded[sort_order]
    reach = 4 * DOC_DEV
    row_block = min(512, total)
    span = row_block + 2 * reach
    edge_ids = jnp.full((reach,), -2, jnp.int32)
    edge_emb = jnp.zeros((reach, feat_dim), embedded.dtype)
    pad_ids = jnp.concatenate([edge_ids, sorted_ids, edge_ids])
    pad_emb = jnp.concatenate([edge_emb, sorted_emb, edge_emb], axis=0)

    def block_max(start):
        row_emb = lax.dynamic_slice_in_dim(sorted_emb, start, row_block, 0)
        row_ids = lax.dynamic_slice_in_dim(sorted_ids, start, row_block, 0)
        col_emb = lax.dynamic_slice_in_dim(pad_emb, start, span, 0)
        col_ids = lax.dynamic_slice_in_dim(pad_ids, start, span, 0)
        duplicate_scores = jnp.einsum('rd,cd->rc', row_emb.astype(jnp.float32), col_emb.astype(jnp.float32))
        row_pos = start + jnp.arange(row_block, dtype=jnp.int32)
        col_pos = start - reach + jnp.arange(span, dtype=jnp.int32)
        match = (row_ids[:, None] == col_ids[None, :]) & (row_pos[:, None] != col_pos[None, :])
        return lax.optimization_barrier(jnp.max(jnp.where(match, duplicate_scores, -1.0), axis=1))
    starts = jnp.arange(total // row_block, dtype=jnp.int32) * row_block
    sorted_max = lax.map(block_max, starts).reshape(total)
    return jnp.zeros((total,), jnp.float32).at[sort_order].set(sorted_max)
```

```python
import functools

import jax
import jax.numpy as jnp
from jax import lax
from jax.experimental import pallas as pl
from jax.experimental.pallas import tpu as pltpu
from jax.sharding import PartitionSpec as P

CL_OWN = 1
LANES = 128
EMPTY = 2.0
VMEM = pl.BlockSpec(memory_space=pltpu.VMEM)
HBM = pl.BlockSpec(memory_space=pltpu.HBM)
PARAMS = pltpu.CompilerParams(vmem_limit_bytes=32 * 2**20)


def iota(shape, dim):
    return lax.broadcasted_iota(jnp.int32, shape, dim)


def in_hbm(array):
    return pltpu.with_memory_space_constraint(array, pltpu.HBM)


def embed_kernel(
    slot_cap, tok_hbm, len_hbm, id_hbm, weight_hbm, bias_hbm,
    packed_ref, place_ref,
    tok, weight, bias, lens, ids, sems,
):
    rows, seq_len, _ = tok.shape
    slots = packed_ref.shape[0]
    pairs = ((len_hbm, lens), (id_hbm, ids), (tok_hbm, tok), (weight_hbm, weight), (bias_hbm, bias))
    copies = [
        pltpu.make_async_copy(source, target, sems.at[at])
        for at, (source, target) in enumerate(pairs)
    ]
    for copy in copies:
        copy.start()
    diagonal = iota((rows, rows), 0) == iota((rows, rows), 1)

    def column(row):
        return jnp.sum(jnp.where(diagonal, row, 0), axis=1, keepdims=True)

    copies[0].wait()
    copies[1].wait()
    counts = column(lens[...])
    owner = ids[...] // CL_OWN
    earlier = (column(owner) == owner) & (iota((rows, rows), 0) < iota((rows, rows), 1))
    rank = jnp.sum(earlier.astype(jnp.int32), axis=0, keepdims=True)
    place_ref[0:1, :] = owner
    place_ref[1:2, :] = rank
    chooser = iota((slots, rows), 0) == owner * slot_cap + rank
    chooser = jnp.where(chooser, 1.0, 0.0)
    empty = jnp.sum(chooser, axis=1, keepdims=True) < 0.5
    copies[2].wait()
    summed = tok[:, 0, :].astype(jnp.float32)
    for t in range(1, seq_len):
        summed += jnp.where(counts > t, tok[:, t, :].astype(jnp.float32), 0.0)
    pooled = (summed / counts.astype(jnp.float32)).astype(jnp.bfloat16)
    copies[3].wait()
    copies[4].wait()
    hidden = jnp.tanh(
        jnp.dot(pooled, weight[...], preferred_element_type=jnp.float32) + bias[...]
    )
    factor = lax.rsqrt(jnp.sum(hidden * hidden, axis=1, keepdims=True) + 1e-06)
    embedded = (hidden * factor).astype(jnp.bfloat16)
    packed = jnp.dot(chooser.astype(jnp.bfloat16), embedded, preferred_element_type=jnp.float32)
    packed_ref[...] = packed.astype(jnp.bfloat16)
    first = packed_ref[:, 0:LANES].astype(jnp.float32)
    first = jnp.where(empty & (iota(first.shape, 1) == 0), EMPTY, first)
    packed_ref[:, 0:LANES] = first.astype(jnp.bfloat16)


def embed(token_states, lengths, cluster_id, proj_weight, proj_bias, owners):
    rows, _, width = token_states.shape
    slot_cap = 2 * rows // owners
    return pl.pallas_call(
        functools.partial(embed_kernel, slot_cap),
        out_shape=(
            jax.ShapeDtypeStruct((owners * slot_cap, width), jnp.bfloat16),
            jax.ShapeDtypeStruct((8, rows), jnp.int32),
        ),
        in_specs=[HBM] * 5,
        out_specs=(VMEM, VMEM),
        scratch_shapes=[
            pltpu.VMEM(token_states.shape, token_states.dtype),
            pltpu.VMEM(proj_weight.shape, proj_weight.dtype),
            pltpu.VMEM((1, width), jnp.float32),
            pltpu.VMEM((1, rows), jnp.int32),
            pltpu.VMEM((1, rows), jnp.int32),
            pltpu.SemaphoreType.DMA((5,)),
        ],
        compiler_params=PARAMS,
        name="embed",
    )(
        in_hbm(token_states),
        in_hbm(lengths.reshape(1, rows)),
        in_hbm(cluster_id.reshape(1, rows)),
        in_hbm(proj_weight),
        in_hbm(proj_bias.reshape(1, width)),
    )


def score_kernel(slot_cap, own_ref, mate_ref, out_ref):
    own = own_ref[...]
    slots = own.shape[0]

    def best(ref, mine):
        scores = lax.dot_general(
            ref[...], own, (((1,), (1,)), ((), ())), preferred_element_type=jnp.float32
        )
        valid = ref[:, 0:LANES][:, 0:1].astype(jnp.float32) < 1.5
        if mine:
            valid = valid & (iota((slots, slots), 0) != iota((slots, slots), 1))
        return jnp.max(jnp.where(valid, scores, -1.0), axis=0, keepdims=True)

    maxima = jnp.maximum(best(own_ref, True), best(mate_ref, False))
    for source in range(slots // slot_cap):
        out_ref[source, :, 0:slot_cap] = maxima[:, source * slot_cap : (source + 1) * slot_cap]


def score(own, mate, owners):
    slot_cap = own.shape[0] // owners
    lanes = -(-slot_cap // LANES) * LANES
    return pl.pallas_call(
        functools.partial(score_kernel, slot_cap),
        out_shape=jax.ShapeDtypeStruct((owners, 1, lanes), jnp.float32),
        in_specs=[VMEM, VMEM],
        out_specs=VMEM,
        compiler_params=PARAMS,
        name="score",
    )(own, mate)


def pick_kernel(returned_ref, place_ref, out_ref):
    owners, _, lanes = returned_ref.shape
    rows = place_ref.shape[1]
    owner = place_ref[0:1, :]
    rank = jnp.broadcast_to(place_ref[1:2, :], (owners, rows))
    returned = returned_ref[...].reshape(owners, lanes)
    taken = jnp.take_along_axis(returned, rank, axis=1, mode="promise_in_bounds")
    taken = jnp.where(iota((owners, rows), 0) == owner, taken, -3.0)
    out_ref[...] = jnp.max(taken, axis=0, keepdims=True)


def pick(returned, place):
    rows = place.shape[1]
    return pl.pallas_call(
        pick_kernel,
        out_shape=jax.ShapeDtypeStruct((1, rows), jnp.float32),
        in_specs=[VMEM, VMEM],
        out_specs=VMEM,
        name="pick",
    )(returned, place).reshape(rows)


def body(token_states, lengths, cluster_id, proj_weight, proj_bias):
    owners = lax.axis_size("docs")
    packed, place = embed(token_states, lengths, cluster_id, proj_weight, proj_bias, owners)
    own = lax.all_to_all(packed, "docs", split_axis=0, concat_axis=0, tiled=True)
    swap = [(i, i ^ 1) for i in range(lax.axis_size("help"))]
    mate = lax.ppermute(own, "help", swap)
    maxima = score(own, mate, owners)
    returned = lax.all_to_all(maxima, "docs", split_axis=0, concat_axis=0, tiled=True)
    return pick(returned, place)


def solution(mesh):
    spread = P(("groups", "docs", "help"))
    in_specs = (P(("groups", "docs", "help"), None, None), spread, spread, P(), P())
    return jax.shard_map(body, mesh=mesh, in_specs=in_specs, out_specs=spread, check_vma=False)
```

```python
import functools

import jax
import jax.numpy as jnp
from jax import lax
from jax.experimental import pallas as pl
from jax.experimental.pallas import tpu as pltpu
from jax.sharding import PartitionSpec as P

CL_OWN = 1
LANES = 128
EMPTY = 2.0
VMEM = pl.BlockSpec(memory_space=pltpu.VMEM)
SMEM = pl.BlockSpec(memory_space=pltpu.SMEM)
HBM = pl.BlockSpec(memory_space=pltpu.HBM)
PARAMS = pltpu.CompilerParams(vmem_limit_bytes=32 * 2**20)

PLAN = (("own", (6, 7)), ("own", (1, 1)), ("own", (7, 6)), ("own", (2, 3)), ("own", (4, 5)), ("own", (3, 2)), ("own", (5, 4)))
GROUPS = ((0,), (1,), (2,), (3,), (4,), (5,), (6,))
AFTER = {}


def iota(shape, dim):
    return lax.broadcasted_iota(jnp.int32, shape, dim)


def in_hbm(array):
    return pltpu.with_memory_space_constraint(array, pltpu.HBM)


def in_vmem(array):
    return pltpu.with_memory_space_constraint(array, pltpu.VMEM)


def rows_of(at, slot_cap, blocks=1):
    return pl.ds(at * slot_cap, blocks * slot_cap)


def layout(core):
    alone = [[steps[core]] for kind, steps in PLAN if kind == "own"]
    keep = [steps[core] for kind, steps in PLAN if kind == "both"]
    give = [steps[1 - core] for kind, steps in PLAN if kind != "own"] + [0]
    return [*alone, keep, give] if keep else [*alone, give]


def embed_kernel(
    slot_cap, block_of, me_ref, core_ref,
    tok_hbm, len_hbm, id_hbm, weight_hbm, bias_hbm, *refs,
):
    *packed_refs, place_ref, tok, weight, bias, lens, ids, sems = refs
    rows, seq_len, _ = tok.shape
    slots = sum(ref.shape[0] for ref in packed_refs)
    pairs = ((len_hbm, lens), (id_hbm, ids), (tok_hbm, tok), (weight_hbm, weight), (bias_hbm, bias))
    copies = [
        pltpu.make_async_copy(source, target, sems.at[at])
        for at, (source, target) in enumerate(pairs)
    ]
    for copy in copies:
        copy.start()
    diagonal = iota((rows, rows), 0) == iota((rows, rows), 1)

    def column(row):
        return jnp.sum(jnp.where(diagonal, row, 0), axis=1, keepdims=True)

    copies[0].wait()
    copies[1].wait()
    counts = column(lens[...])
    owner = ids[...] // CL_OWN
    earlier = (column(owner) == owner) & (iota((rows, rows), 0) < iota((rows, rows), 1))
    rank = jnp.sum(earlier.astype(jnp.int32), axis=0, keepdims=True)
    place_ref[0:1, :] = owner
    place_ref[1:2, :] = rank
    block = block_of(owner, me_ref, core_ref)
    chooser = iota((slots, rows), 0) == block * slot_cap + rank
    chooser = jnp.where(chooser, 1.0, 0.0)
    empty = jnp.sum(chooser, axis=1, keepdims=True) < 0.5
    copies[2].wait()
    summed = tok[:, 0, :].astype(jnp.float32)
    for t in range(1, seq_len):
        summed += jnp.where(counts > t, tok[:, t, :].astype(jnp.float32), 0.0)
    pooled = (summed / counts.astype(jnp.float32)).astype(jnp.bfloat16)
    copies[3].wait()
    copies[4].wait()
    hidden = jnp.tanh(
        jnp.dot(pooled, weight[...], preferred_element_type=jnp.float32) + bias[...]
    )
    factor = lax.rsqrt(jnp.sum(hidden * hidden, axis=1, keepdims=True) + 1e-06)
    embedded = (hidden * factor).astype(jnp.bfloat16)
    packed = jnp.dot(chooser.astype(jnp.bfloat16), embedded, preferred_element_type=jnp.float32)
    first = packed[:, 0:LANES]
    first = jnp.where(empty & (iota(first.shape, 1) == 0), EMPTY, first).astype(jnp.bfloat16)
    rest = packed[:, LANES:].astype(jnp.bfloat16)
    at = 0
    for ref in packed_refs:
        ref[:, 0:LANES] = first[at : at + ref.shape[0]]
        ref[:, LANES:] = rest[at : at + ref.shape[0]]
        at += ref.shape[0]


def plan_block(owner, me_ref, core_ref):
    step = owner ^ me_ref[0]
    block = jnp.zeros_like(step)
    flat = [sum(layout(core), []) for core in range(2)]
    for at in range(len(flat[0])):
        block = jnp.where(step == jnp.where(core_ref[0] == 0, flat[0][at], flat[1][at]), at, block)
    return block


def embed(me, core, arrays, sizes, slot_cap, block_of):
    token_states, lengths, cluster_id, proj_weight, proj_bias = arrays
    rows, _, width = token_states.shape
    return pl.pallas_call(
        functools.partial(embed_kernel, slot_cap, block_of),
        out_shape=[jax.ShapeDtypeStruct((size, width), jnp.bfloat16) for size in sizes]
        + [jax.ShapeDtypeStruct((8, rows), jnp.int32)],
        in_specs=[SMEM] * 2 + [HBM] * 5,
        out_specs=[VMEM] * (len(sizes) + 1),
        scratch_shapes=[
            pltpu.VMEM(token_states.shape, token_states.dtype),
            pltpu.VMEM(proj_weight.shape, proj_weight.dtype),
            pltpu.VMEM((1, width), jnp.float32),
            pltpu.VMEM((1, rows), jnp.int32),
            pltpu.VMEM((1, rows), jnp.int32),
            pltpu.SemaphoreType.DMA((5,)),
        ],
        compiler_params=PARAMS,
        name="embed",
    )(
        me,
        core,
        in_hbm(token_states),
        in_hbm(lengths.reshape(1, rows)),
        in_hbm(cluster_id.reshape(1, rows)),
        in_hbm(proj_weight),
        in_hbm(proj_bias.reshape(1, width)),
    )


def move_kernel(count, moves, core_ref, *refs):
    in_refs, out_refs = refs[:count], refs[len(refs) - len(moves[0]) :]
    for core in range(2):

        @pl.when(core_ref[0] == core)
        def _():
            for ref, parts in zip(out_refs, moves[core]):
                at = 0
                for source, part in parts:
                    size = part.size
                    ref[pl.ds(at, size), :] = in_refs[source][part, :]
                    at += size


def move(core, values, moves, name, after=()):
    width, kind = values[0].shape[1], values[0].dtype
    sizes = [sum(part.size for _, part in parts) for parts in moves[0]]
    return pl.pallas_call(
        functools.partial(move_kernel, len(values), moves),
        out_shape=[jax.ShapeDtypeStruct((size, width), kind) for size in sizes],
        in_specs=[SMEM] + [VMEM] * (len(values) + len(after)),
        out_specs=[VMEM] * len(sizes),
        compiler_params=PARAMS,
        name=name,
    )(core, *values, *after)


def best_of(ref, columns, same):
    scores = lax.dot_general(
        ref[...], columns, (((1,), (1,)), ((), ())), preferred_element_type=jnp.float32
    )
    valid = ref[:, 0:LANES].astype(jnp.float32)[:, 0:1] < 1.5
    if same:
        valid = valid & (iota(scores.shape, 0) != iota(scores.shape, 1))
    return jnp.max(jnp.where(valid, scores, -1.0), axis=0, keepdims=True)


def write_maxima(out_ref, mine, other, sources, slot_cap):
    columns = mine[...]
    maxima = jnp.maximum(best_of(mine, columns, True), best_of(other, columns, False))
    for at, source in enumerate(sources):
        out_ref[source, :, 0:slot_cap] = maxima[:, at * slot_cap : (at + 1) * slot_cap]


def score_kernel(slot_cap, me_ref, core_ref, give_ref, got_ref, *refs):
    *parts, out_ref, mine, other = refs
    received, handed = parts[: len(PLAN)], parts[len(PLAN) :]
    own = rows_of(give_ref.shape[0] // slot_cap - 1, slot_cap)
    places = [((0, 0), [((give_ref, own), (got_ref, own))] * 2)]
    offsets = {}
    for group, members in enumerate(GROUPS):
        at = 0
        for op in members:
            offsets[op] = (handed[group], at)
            at += 2 if PLAN[op][0] == "both" else 1
    for op, (kind, steps) in enumerate(PLAN):
        ours = (received[op], rows_of(0, slot_cap))
        theirs = (offsets[op][0], rows_of(offsets[op][1], slot_cap))
        if kind == "own":
            places.append((steps, [(ours, theirs)] * 2))
        elif kind == "mate":
            places.append((steps[::-1], [(theirs, ours)] * 2))
        else:
            for (ref, start), order in (((received[op], 0), steps), (offsets[op], steps[::-1])):
                pair = [(ref, rows_of(start + core, slot_cap)) for core in range(2)]
                places.append((order, [(pair[core], pair[1 - core]) for core in range(2)]))
    for core in range(2):

        @pl.when(core_ref[0] == core)
        def _():
            for at, (_, by_core) in enumerate(places):
                (ours, our_rows), (theirs, their_rows) = by_core[core]
                mine[rows_of(at, slot_cap), :] = ours[our_rows, :]
                other[rows_of(at, slot_cap), :] = theirs[their_rows, :]

    sources = [me_ref[0] ^ jnp.where(core_ref[0] == 0, *steps) for steps, _ in places]
    write_maxima(out_ref, mine, other, sources, slot_cap)


def score(me, core, give, got, parts, owners, slot_cap):
    width = give.shape[1]
    lanes = -(-slot_cap // LANES) * LANES
    return pl.pallas_call(
        functools.partial(score_kernel, slot_cap),
        out_shape=jax.ShapeDtypeStruct((owners, 1, lanes), jnp.float32),
        in_specs=[SMEM] * 2 + [VMEM] * (2 + len(parts)),
        out_specs=VMEM,
        scratch_shapes=[pltpu.VMEM((owners * slot_cap, width), give.dtype)] * 2,
        compiler_params=PARAMS,
        name="score",
    )(me, core, give, got, *parts)


def plain_score_kernel(slot_cap, mine_ref, other_ref, out_ref):
    write_maxima(out_ref, mine_ref, other_ref, range(out_ref.shape[0]), slot_cap)


def plain_score(mine, other, owners, slot_cap):
    lanes = -(-slot_cap // LANES) * LANES
    return pl.pallas_call(
        functools.partial(plain_score_kernel, slot_cap),
        out_shape=jax.ShapeDtypeStruct((owners, 1, lanes), jnp.float32),
        in_specs=[VMEM, VMEM],
        out_specs=VMEM,
        compiler_params=PARAMS,
        name="score",
    )(mine, other)


def pick_kernel(returned_ref, place_ref, out_ref):
    owners, _, lanes = returned_ref.shape
    rows = place_ref.shape[1]
    owner = place_ref[0:1, :]
    rank = jnp.broadcast_to(place_ref[1:2, :], (owners, rows))
    returned = returned_ref[...].reshape(owners, lanes)
    taken = jnp.take_along_axis(returned, rank, axis=1, mode="promise_in_bounds")
    taken = jnp.where(iota((owners, rows), 0) == owner, taken, -3.0)
    out_ref[...] = jnp.max(taken, axis=0, keepdims=True)


def pick(returned, place):
    rows = place.shape[1]
    return pl.pallas_call(
        pick_kernel,
        out_shape=jax.ShapeDtypeStruct((1, rows), jnp.float32),
        in_specs=[VMEM, VMEM],
        out_specs=VMEM,
        name="pick",
    )(in_vmem(returned), in_vmem(place)).reshape(rows)


def step_to(value, steps):
    helpers = lax.axis_size("help")
    pairs = [
        (doc * helpers + core, (doc ^ steps[core]) * helpers + core)
        for doc in range(lax.axis_size("docs"))
        for core in range(helpers)
    ]
    return lax.ppermute(value, ("docs", "help"), pairs)


def swap(value):
    return lax.ppermute(value, "help", [(i, i ^ 1) for i in range(lax.axis_size("help"))])


def planned_scores(me, core, arrays, owners, slot_cap):
    sizes = [len(steps) * slot_cap for steps in layout(0)]
    *packed, place = embed(me, core, arrays, sizes, slot_cap, plan_block)
    alone = iter(packed)
    give = packed[-1]
    keep = packed[-2]
    got = swap(give)
    merged, at_keep, at_got = {}, 0, 0
    wanted = {}
    for op, (kind, _) in enumerate(PLAN):
        wait = AFTER.get(op, ())
        if kind == "own":
            merged[op] = next(alone)
            if wait:
                wanted.setdefault(wait, []).append((op, "own", None, None))
            continue
        wanted.setdefault(wait, []).append((op, kind, at_keep, at_got))
        at_got += 1
        at_keep += kind == "both"
    received = {}

    def send(op):
        received[op] = step_to(merged[op], PLAN[op][1])

    for op in range(len(PLAN)):
        if PLAN[op][0] == "own" and not AFTER.get(op, ()):
            send(op)
    for wait, ops in wanted.items():
        values = [keep, got]
        moves = [[], []]
        for op, kind, from_keep, from_got in ops:
            if kind == "own":
                values.append(merged[op])
                for core_moves in moves:
                    core_moves.append([(len(values) - 1, rows_of(0, slot_cap))])
                continue
            theirs = (1, rows_of(from_got, slot_cap))
            if kind == "mate":
                for core_moves in moves:
                    core_moves.append([theirs])
                continue
            ours = (0, rows_of(from_keep, slot_cap))
            moves[0].append([ours, theirs])
            moves[1].append([theirs, ours])
        outs = move(core, values, moves, "merge", [received[op] for op in wait])
        for (op, *_), out in zip(ops, outs):
            merged[op] = out
            send(op)
    handed = []
    for members in GROUPS:
        values = [received[op] for op in members]
        if len(values) > 1:
            parts = [(at, pl.ds(0, value.shape[0])) for at, value in enumerate(values)]
            (joined,) = move(core, values, [[parts], [parts]], "join")
        else:
            joined = values[0]
        handed.append(swap(joined))
    parts = [received[op] for op in range(len(PLAN))] + handed
    return score(me, core, give, got, parts, owners, slot_cap), place


def plain_scores(me, core, arrays, owners, slot_cap):
    packed, place = embed(
        me, core, arrays, [owners * slot_cap], slot_cap, lambda owner, *_: owner
    )
    mine = lax.all_to_all(packed, "docs", split_axis=0, concat_axis=0, tiled=True)
    return plain_score(mine, swap(mine), owners, slot_cap), place


def body(*arrays):
    owners = lax.axis_size("docs")
    slot_cap = 2 * arrays[0].shape[0] // owners
    me = lax.axis_index("docs").reshape(1)
    core = lax.axis_index("help").reshape(1)
    planned = sum(len(steps) for steps in layout(0)) == owners
    scores = planned_scores if planned else plain_scores
    maxima, place = scores(me, core, arrays, owners, slot_cap)
    returned = lax.all_to_all(maxima, "docs", split_axis=0, concat_axis=0, tiled=True)
    return pick(returned, place)


def solution(mesh):
    spread = P(("groups", "docs", "help"))
    in_specs = (P(("groups", "docs", "help"), None, None), spread, spread, P(), P())
    return jax.shard_map(body, mesh=mesh, in_specs=in_specs, out_specs=spread, check_vma=False)
```

```python
import functools

import jax
import jax.numpy as jnp
from jax import lax
from jax.experimental import pallas as pl
from jax.experimental.pallas import tpu as pltpu
from jax.sharding import PartitionSpec as P

CL_OWN = 1
LANES = 128
EMPTY = 2.0
VMEM = pl.BlockSpec(memory_space=pltpu.VMEM)
SMEM = pl.BlockSpec(memory_space=pltpu.SMEM)
HBM = pl.BlockSpec(memory_space=pltpu.HBM)
PARAMS = pltpu.CompilerParams(vmem_limit_bytes=32 * 2**20)

ORDER = ((6, 1, 7, 2, 4, 3, 5), (6, 1, 7, 2, 4, 3, 5))


def iota(shape, dim):
    return lax.broadcasted_iota(jnp.int32, shape, dim)


def in_hbm(array):
    return pltpu.with_memory_space_constraint(array, pltpu.HBM)


def in_vmem(array):
    return pltpu.with_memory_space_constraint(array, pltpu.VMEM)


def embed_kernel(
    slot_cap, block_of, me_ref, core_ref,
    tok_hbm, len_hbm, id_hbm, weight_hbm, bias_hbm, *refs,
):
    *packed_refs, place_ref, tok, weight, bias, lens, ids, sems = refs
    rows, seq_len, _ = tok.shape
    slots = sum(ref.shape[0] for ref in packed_refs)
    pairs = ((len_hbm, lens), (id_hbm, ids), (tok_hbm, tok), (weight_hbm, weight), (bias_hbm, bias))
    copies = [
        pltpu.make_async_copy(source, target, sems.at[at])
        for at, (source, target) in enumerate(pairs)
    ]
    for copy in copies:
        copy.start()
    diagonal = iota((rows, rows), 0) == iota((rows, rows), 1)

    def column(row):
        return jnp.sum(jnp.where(diagonal, row, 0), axis=1, keepdims=True)

    copies[0].wait()
    copies[1].wait()
    counts = column(lens[...])
    owner = ids[...] // CL_OWN
    earlier = (column(owner) == owner) & (iota((rows, rows), 0) < iota((rows, rows), 1))
    rank = jnp.sum(earlier.astype(jnp.int32), axis=0, keepdims=True)
    place_ref[0:1, :] = owner
    place_ref[1:2, :] = rank
    block = block_of(owner, me_ref, core_ref)
    chooser = iota((slots, rows), 0) == block * slot_cap + rank
    chooser = jnp.where(chooser, 1.0, 0.0)
    empty = jnp.sum(chooser, axis=1, keepdims=True) < 0.5
    copies[2].wait()
    summed = tok[:, 0, :].astype(jnp.float32)
    for t in range(1, seq_len):
        summed += jnp.where(counts > t, tok[:, t, :].astype(jnp.float32), 0.0)
    pooled = (summed / counts.astype(jnp.float32)).astype(jnp.bfloat16)
    copies[3].wait()
    copies[4].wait()
    hidden = jnp.tanh(
        jnp.dot(pooled, weight[...], preferred_element_type=jnp.float32) + bias[...]
    )
    factor = lax.rsqrt(jnp.sum(hidden * hidden, axis=1, keepdims=True) + 1e-06)
    embedded = (hidden * factor).astype(jnp.bfloat16)
    packed = jnp.dot(chooser.astype(jnp.bfloat16), embedded, preferred_element_type=jnp.float32)
    first = packed[:, 0:LANES]
    first = jnp.where(empty & (iota(first.shape, 1) == 0), EMPTY, first).astype(jnp.bfloat16)
    rest = packed[:, LANES:].astype(jnp.bfloat16)
    at = 0
    for ref in packed_refs:
        ref[:, 0:LANES] = first[at : at + ref.shape[0]]
        ref[:, LANES:] = rest[at : at + ref.shape[0]]
        at += ref.shape[0]


def order_block(owner, me_ref, core_ref):
    step = owner ^ me_ref[0]
    block = jnp.zeros_like(step)
    for at, steps in enumerate(zip(*ORDER), 1):
        block = jnp.where(step == jnp.where(core_ref[0] == 0, *steps), at, block)
    return block


def owner_block(owner, *_):
    return owner


def embed(me, core, arrays, sizes, slot_cap, block_of):
    token_states, lengths, cluster_id, proj_weight, proj_bias = arrays
    rows, _, width = token_states.shape
    return pl.pallas_call(
        functools.partial(embed_kernel, slot_cap, block_of),
        out_shape=[jax.ShapeDtypeStruct((size, width), jnp.bfloat16) for size in sizes]
        + [jax.ShapeDtypeStruct((8, rows), jnp.int32)],
        in_specs=[SMEM] * 2 + [HBM] * 5,
        out_specs=[VMEM] * (len(sizes) + 1),
        scratch_shapes=[
            pltpu.VMEM(token_states.shape, token_states.dtype),
            pltpu.VMEM(proj_weight.shape, proj_weight.dtype),
            pltpu.VMEM((1, width), jnp.float32),
            pltpu.VMEM((1, rows), jnp.int32),
            pltpu.VMEM((1, rows), jnp.int32),
            pltpu.SemaphoreType.DMA((5,)),
        ],
        compiler_params=PARAMS,
        name="embed",
    )(
        me,
        core,
        in_hbm(token_states),
        in_hbm(lengths.reshape(1, rows)),
        in_hbm(cluster_id.reshape(1, rows)),
        in_hbm(proj_weight),
        in_hbm(proj_bias.reshape(1, width)),
    )


def join_kernel(*refs):
    *in_refs, out_ref = refs
    at = 0
    for ref in in_refs:
        out_ref[pl.ds(at, ref.shape[0]), :] = ref[...]
        at += ref.shape[0]


def join(blocks):
    rows = sum(block.shape[0] for block in blocks)
    return pl.pallas_call(
        join_kernel,
        out_shape=jax.ShapeDtypeStruct((rows, blocks[0].shape[1]), blocks[0].dtype),
        in_specs=[VMEM] * len(blocks),
        out_specs=VMEM,
        compiler_params=PARAMS,
        name="join",
    )(*blocks)


def best_of(ref, columns, same):
    scores = lax.dot_general(
        ref[...], columns, (((1,), (1,)), ((), ())), preferred_element_type=jnp.float32
    )
    valid = ref[:, 0:LANES].astype(jnp.float32)[:, 0:1] < 1.5
    if same:
        valid = valid & (iota(scores.shape, 0) != iota(scores.shape, 1))
    return jnp.max(jnp.where(valid, scores, -1.0), axis=0, keepdims=True)


def score_kernel(slot_cap, sources_of, me_ref, core_ref, mine_ref, other_ref, out_ref):
    columns = mine_ref[...]
    maxima = jnp.maximum(best_of(mine_ref, columns, True), best_of(other_ref, columns, False))
    for at, source in enumerate(sources_of(out_ref.shape[0], me_ref, core_ref)):
        out_ref[source, :, 0:slot_cap] = maxima[:, at * slot_cap : (at + 1) * slot_cap]


def order_sources(owners, me_ref, core_ref):
    steps = [jnp.where(core_ref[0] == 0, *steps) for steps in zip(*ORDER)]
    return [me_ref[0]] + [me_ref[0] ^ step for step in steps]


def owner_sources(owners, *_):
    return range(owners)


def score(me, core, mine, other, owners, slot_cap, sources_of):
    lanes = -(-slot_cap // LANES) * LANES
    return pl.pallas_call(
        functools.partial(score_kernel, slot_cap, sources_of),
        out_shape=jax.ShapeDtypeStruct((owners, 1, lanes), jnp.float32),
        in_specs=[SMEM] * 2 + [VMEM] * 2,
        out_specs=VMEM,
        compiler_params=PARAMS,
        name="score",
    )(me, core, mine, other)


def pick_kernel(returned_ref, place_ref, out_ref):
    owners, _, lanes = returned_ref.shape
    rows = place_ref.shape[1]
    owner = place_ref[0:1, :]
    rank = jnp.broadcast_to(place_ref[1:2, :], (owners, rows))
    returned = returned_ref[...].reshape(owners, lanes)
    taken = jnp.take_along_axis(returned, rank, axis=1, mode="promise_in_bounds")
    taken = jnp.where(iota((owners, rows), 0) == owner, taken, -3.0)
    out_ref[...] = jnp.max(taken, axis=0, keepdims=True)


def pick(returned, place):
    rows = place.shape[1]
    return pl.pallas_call(
        pick_kernel,
        out_shape=jax.ShapeDtypeStruct((1, rows), jnp.float32),
        in_specs=[VMEM, VMEM],
        out_specs=VMEM,
        name="pick",
    )(in_vmem(returned), in_vmem(place)).reshape(rows)


def step_to(value, steps):
    helpers = lax.axis_size("help")
    pairs = [
        (doc * helpers + core, (doc ^ steps[core]) * helpers + core)
        for doc in range(lax.axis_size("docs"))
        for core in range(helpers)
    ]
    return lax.ppermute(value, ("docs", "help"), pairs)


def swap(value):
    return lax.ppermute(value, "help", [(i, i ^ 1) for i in range(lax.axis_size("help"))])


def body(*arrays):
    owners = lax.axis_size("docs")
    slot_cap = 2 * arrays[0].shape[0] // owners
    me = lax.axis_index("docs").reshape(1)
    core = lax.axis_index("help").reshape(1)
    if owners == len(ORDER[0]) + 1:
        block_of, sources_of = order_block, order_sources
        own, *blocks, place = embed(me, core, arrays, [slot_cap] * owners, slot_cap, block_of)
        mine = join([own] + [step_to(*send) for send in zip(blocks, zip(*ORDER))])
    else:
        block_of, sources_of = owner_block, owner_sources
        packed, place = embed(me, core, arrays, [owners * slot_cap], slot_cap, block_of)
        mine = lax.all_to_all(packed, "docs", split_axis=0, concat_axis=0, tiled=True)
    maxima = score(me, core, mine, swap(mine), owners, slot_cap, sources_of)
    returned = lax.all_to_all(maxima, "docs", split_axis=0, concat_axis=0, tiled=True)
    return pick(returned, place)


def solution(mesh):
    spread = P(("groups", "docs", "help"))
    in_specs = (P(("groups", "docs", "help"), None, None), spread, spread, P(), P())
    return jax.shard_map(body, mesh=mesh, in_specs=in_specs, out_specs=spread, check_vma=False)
```

```python
import functools

import jax
import jax.numpy as jnp
from jax import lax
from jax.experimental import pallas as pl
from jax.experimental.pallas import tpu as pltpu
from jax.sharding import PartitionSpec as P

CL_OWN = 1
LANES = 128
EMPTY = 2.0
WEIGHT_PARTS = 8
VMEM = pl.BlockSpec(memory_space=pltpu.VMEM)
SMEM = pl.BlockSpec(memory_space=pltpu.SMEM)
HBM = pl.BlockSpec(memory_space=pltpu.HBM)
PARAMS = pltpu.CompilerParams(vmem_limit_bytes=32 * 2**20)

ORDER = ((6, 1, 7, 2, 4, 3, 5), (6, 1, 7, 2, 4, 3, 5))


def turn(doc):
    return (doc >> 2) & 1


def kind(doc):
    return ((doc >> 1) ^ (doc >> 2)) & 1


def iota(shape, dim):
    return lax.broadcasted_iota(jnp.int32, shape, dim)


def in_hbm(array):
    return pltpu.with_memory_space_constraint(array, pltpu.HBM)


def in_vmem(array):
    return pltpu.with_memory_space_constraint(array, pltpu.VMEM)


def embed_kernel(
    slot_cap, block_of, me_ref,
    tok_hbm, len_hbm, id_hbm, weight_hbm, bias_hbm, *refs,
):
    *packed_refs, place_ref, tok, weight, bias, lens, ids, sems = refs
    rows, seq_len, _ = tok.shape
    slots = sum(ref.shape[0] for ref in packed_refs)
    pairs = [(len_hbm, lens), (id_hbm, ids), (tok_hbm, tok), (bias_hbm, bias)]
    part = weight.shape[0] // WEIGHT_PARTS
    for at in range(WEIGHT_PARTS):
        pairs.append((weight_hbm.at[pl.ds(at * part, part)], weight.at[pl.ds(at * part, part)]))
    copies = [
        pltpu.make_async_copy(source, target, sems.at[at])
        for at, (source, target) in enumerate(pairs)
    ]
    for copy in copies:
        copy.start()
    diagonal = iota((rows, rows), 0) == iota((rows, rows), 1)

    def column(row):
        return jnp.sum(jnp.where(diagonal, row, 0), axis=1, keepdims=True)

    copies[0].wait()
    copies[1].wait()
    counts = column(lens[...])
    owner = ids[...] // CL_OWN
    earlier = (column(owner) == owner) & (iota((rows, rows), 0) < iota((rows, rows), 1))
    rank = jnp.sum(earlier.astype(jnp.int32), axis=0, keepdims=True)
    place_ref[0:1, :] = owner
    place_ref[1:2, :] = rank
    block = block_of(owner, me_ref[0])
    chooser = iota((slots, rows), 0) == block * slot_cap + rank
    chooser = jnp.where(chooser, 1.0, 0.0)
    empty = jnp.sum(chooser, axis=1, keepdims=True) < 0.5
    copies[2].wait()
    summed = tok[:, 0, :].astype(jnp.float32)
    for t in range(1, seq_len):
        summed += jnp.where(counts > t, tok[:, t, :].astype(jnp.float32), 0.0)
    pooled = (summed / counts.astype(jnp.float32)).astype(jnp.bfloat16)
    for copy in copies[3:]:
        copy.wait()
    hidden = jnp.tanh(
        jnp.dot(pooled, weight[...], preferred_element_type=jnp.float32) + bias[...]
    )
    factor = lax.rsqrt(jnp.sum(hidden * hidden, axis=1, keepdims=True) + 1e-06)
    embedded = (hidden * factor).astype(jnp.bfloat16)
    packed = jnp.dot(chooser.astype(jnp.bfloat16), embedded, preferred_element_type=jnp.float32)
    first = packed[:, 0:LANES]
    first = jnp.where(empty & (iota(first.shape, 1) == 0), EMPTY, first).astype(jnp.bfloat16)
    rest = packed[:, LANES:].astype(jnp.bfloat16)
    at = 0
    for ref in packed_refs:
        ref[:, 0:LANES] = first[at : at + ref.shape[0]]
        ref[:, LANES:] = rest[at : at + ref.shape[0]]
        at += ref.shape[0]


def order_block(owner, me):
    step = owner ^ me
    block = jnp.zeros_like(step)
    for at, steps in enumerate(zip(*ORDER), 1):
        block = jnp.where(step == jnp.where(kind(me) == 0, *steps), at, block)
    return block


def owner_block(owner, _):
    return owner


def embed(me, arrays, sizes, slot_cap, block_of):
    token_states, lengths, cluster_id, proj_weight, proj_bias = arrays
    rows, _, width = token_states.shape
    return pl.pallas_call(
        functools.partial(embed_kernel, slot_cap, block_of),
        out_shape=[jax.ShapeDtypeStruct((size, width), jnp.bfloat16) for size in sizes]
        + [jax.ShapeDtypeStruct((8, rows), jnp.int32)],
        in_specs=[SMEM] + [HBM] * 5,
        out_specs=[VMEM] * (len(sizes) + 1),
        scratch_shapes=[
            pltpu.VMEM(token_states.shape, token_states.dtype),
            pltpu.VMEM(proj_weight.shape, proj_weight.dtype),
            pltpu.VMEM((1, width), jnp.float32),
            pltpu.VMEM((1, rows), jnp.int32),
            pltpu.VMEM((1, rows), jnp.int32),
            pltpu.SemaphoreType.DMA((4 + WEIGHT_PARTS,)),
        ],
        compiler_params=PARAMS,
        name="embed",
    )(
        me,
        in_hbm(token_states),
        in_hbm(lengths.reshape(1, rows)),
        in_hbm(cluster_id.reshape(1, rows)),
        in_hbm(proj_weight),
        in_hbm(proj_bias.reshape(1, width)),
    )


def join_kernel(*refs):
    *in_refs, out_ref = refs
    at = 0
    for ref in in_refs:
        out_ref[pl.ds(at, ref.shape[0]), :] = ref[...]
        at += ref.shape[0]


def join(blocks):
    rows = sum(block.shape[0] for block in blocks)
    return pl.pallas_call(
        join_kernel,
        out_shape=jax.ShapeDtypeStruct((rows, blocks[0].shape[1]), blocks[0].dtype),
        in_specs=[VMEM] * len(blocks),
        out_specs=VMEM,
        compiler_params=PARAMS,
        name="join",
    )(*blocks)


def best_of(scores, rows):
    valid = rows[:, 0:LANES].astype(jnp.float32)[:, 0:1] < 1.5
    return jnp.max(jnp.where(valid, scores, -1.0), axis=0, keepdims=True)


def inner_kernel(mine_ref, best_ref, turned_ref):
    turned = mine_ref[...].T
    turned_ref[...] = turned
    scores = jnp.dot(mine_ref[...], turned, preferred_element_type=jnp.float32)
    itself = iota(scores.shape, 0) == iota(scores.shape, 1)
    best_ref[...] = best_of(jnp.where(itself, -1.0, scores), mine_ref)


def inner_best(mine):
    slots, width = mine.shape
    return pl.pallas_call(
        inner_kernel,
        out_shape=(
            jax.ShapeDtypeStruct((1, slots), jnp.float32),
            jax.ShapeDtypeStruct((width, slots), mine.dtype),
        ),
        in_specs=[VMEM],
        out_specs=(VMEM, VMEM),
        compiler_params=PARAMS,
        name="inner",
    )(mine)


def score_kernel(slot_cap, sources_of, me_ref, best_ref, turned_ref, other_ref, out_ref):
    scores = jnp.dot(other_ref[...], turned_ref[...], preferred_element_type=jnp.float32)
    maxima = jnp.maximum(best_ref[...], best_of(scores, other_ref))
    for at, source in enumerate(sources_of(out_ref.shape[0], me_ref[0])):
        out_ref[source, :, 0:slot_cap] = maxima[:, at * slot_cap : (at + 1) * slot_cap]


def order_sources(owners, me):
    return [me] + [me ^ jnp.where(kind(me) == 0, *steps) for steps in zip(*ORDER)]


def owner_sources(owners, _):
    return range(owners)


def score(me, mine, other, owners, slot_cap, sources_of):
    lanes = -(-slot_cap // LANES) * LANES
    return pl.pallas_call(
        functools.partial(score_kernel, slot_cap, sources_of),
        out_shape=jax.ShapeDtypeStruct((owners, 1, lanes), jnp.float32),
        in_specs=[SMEM] + [VMEM] * 3,
        out_specs=VMEM,
        compiler_params=PARAMS,
        name="score",
    )(me, *inner_best(mine), other)


def pick_kernel(returned_ref, place_ref, out_ref):
    owners, _, lanes = returned_ref.shape
    rows = place_ref.shape[1]
    owner = place_ref[0:1, :]
    rank = jnp.broadcast_to(place_ref[1:2, :], (owners, rows))
    returned = returned_ref[...].reshape(owners, lanes)
    taken = jnp.take_along_axis(returned, rank, axis=1, mode="promise_in_bounds")
    taken = jnp.where(iota((owners, rows), 0) == owner, taken, -3.0)
    out_ref[...] = jnp.max(taken, axis=0, keepdims=True)


def pick(returned, place):
    rows = place.shape[1]
    return pl.pallas_call(
        pick_kernel,
        out_shape=jax.ShapeDtypeStruct((1, rows), jnp.float32),
        in_specs=[VMEM, VMEM],
        out_specs=VMEM,
        name="pick",
    )(in_vmem(returned), in_vmem(place)).reshape(rows)


def rows_of_devices(helpers, docs):
    return [[doc * helpers + (row ^ turn(doc)) for doc in range(docs)] for row in range(helpers)]


def step_to(value, steps):
    rows = rows_of_devices(lax.axis_size("help"), lax.axis_size("docs"))
    pairs = [
        (row[doc], row[doc ^ steps[kind(doc)]]) for row in rows for doc in range(len(row))
    ]
    return lax.ppermute(value, ("docs", "help"), pairs)


def exchange(value):
    rows = rows_of_devices(lax.axis_size("help"), lax.axis_size("docs"))
    return lax.all_to_all(
        value, ("docs", "help"), split_axis=0, concat_axis=0, tiled=True, axis_index_groups=rows
    )


def swap(value):
    return lax.ppermute(value, "help", [(i, i ^ 1) for i in range(lax.axis_size("help"))])


def body(*arrays):
    owners = lax.axis_size("docs")
    slot_cap = 2 * arrays[0].shape[0] // owners
    me = lax.axis_index("docs").reshape(1)
    if owners == len(ORDER[0]) + 1:
        block_of, sources_of = order_block, order_sources
        own, *blocks, place = embed(me, arrays, [slot_cap] * owners, slot_cap, block_of)
        mine = join([own] + [step_to(*send) for send in zip(blocks, zip(*ORDER))])
    else:
        block_of, sources_of = owner_block, owner_sources
        packed, place = embed(me, arrays, [owners * slot_cap], slot_cap, block_of)
        mine = exchange(packed)
    maxima = score(me, mine, swap(mine), owners, slot_cap, sources_of)
    returned = exchange(maxima)
    return pick(returned, place)


def solution(mesh):
    spread = P(("groups", "docs", "help"))
    in_specs = (P(("groups", "docs", "help"), None, None), spread, spread, P(), P())
    return jax.shard_map(body, mesh=mesh, in_specs=in_specs, out_specs=spread, check_vma=False)
```

```python
import functools

import jax
import jax.numpy as jnp
from jax import lax
from jax.experimental import pallas as pl
from jax.experimental.pallas import tpu as pltpu
from jax.sharding import PartitionSpec as P

CL_OWN = 1
LANES = 128
EMPTY = 2.0
WEIGHT_PARTS = 8
VMEM = pl.BlockSpec(memory_space=pltpu.VMEM)
SMEM = pl.BlockSpec(memory_space=pltpu.SMEM)
HBM = pl.BlockSpec(memory_space=pltpu.HBM)
PARAMS = pltpu.CompilerParams(vmem_limit_bytes=32 * 2**20)

ORDER = (6, 1, 7, 2, 5, 3, 4)


def turn(doc):
    return (doc >> 2) & 1


def iota(shape, dim):
    return lax.broadcasted_iota(jnp.int32, shape, dim)


def in_hbm(array):
    return pltpu.with_memory_space_constraint(array, pltpu.HBM)


def in_vmem(array):
    return pltpu.with_memory_space_constraint(array, pltpu.VMEM)


def embed_kernel(
    slot_cap, block_of, me_ref,
    tok_hbm, len_hbm, id_hbm, weight_hbm, bias_hbm, *refs,
):
    *packed_refs, place_ref, tok, weight, bias, lens, ids, sems = refs
    rows, seq_len, _ = tok.shape
    slots = sum(ref.shape[0] for ref in packed_refs)
    pairs = [(len_hbm, lens), (id_hbm, ids), (tok_hbm, tok), (bias_hbm, bias)]
    part = weight.shape[0] // WEIGHT_PARTS
    for at in range(WEIGHT_PARTS):
        pairs.append((weight_hbm.at[pl.ds(at * part, part)], weight.at[pl.ds(at * part, part)]))
    copies = [
        pltpu.make_async_copy(source, target, sems.at[at])
        for at, (source, target) in enumerate(pairs)
    ]
    for copy in copies:
        copy.start()
    diagonal = iota((rows, rows), 0) == iota((rows, rows), 1)

    def column(row):
        return jnp.sum(jnp.where(diagonal, row, 0), axis=1, keepdims=True)

    copies[0].wait()
    copies[1].wait()
    counts = column(lens[...])
    owner = ids[...] // CL_OWN
    earlier = (column(owner) == owner) & (iota((rows, rows), 0) < iota((rows, rows), 1))
    rank = jnp.sum(earlier.astype(jnp.int32), axis=0, keepdims=True)
    place_ref[0:1, :] = owner
    place_ref[1:2, :] = rank
    block = block_of(owner, me_ref[0])
    chooser = iota((slots, rows), 0) == block * slot_cap + rank
    chooser = jnp.where(chooser, 1.0, 0.0)
    empty = jnp.sum(chooser, axis=1, keepdims=True) < 0.5
    copies[2].wait()
    summed = tok[:, 0, :].astype(jnp.float32)
    for t in range(1, seq_len):
        summed += jnp.where(counts > t, tok[:, t, :].astype(jnp.float32), 0.0)
    pooled = (summed / counts.astype(jnp.float32)).astype(jnp.bfloat16)
    for copy in copies[3:]:
        copy.wait()
    hidden = jnp.tanh(
        jnp.dot(pooled, weight[...], preferred_element_type=jnp.float32) + bias[...]
    )
    factor = lax.rsqrt(jnp.sum(hidden * hidden, axis=1, keepdims=True) + 1e-06)
    embedded = (hidden * factor).astype(jnp.bfloat16)
    packed = jnp.dot(chooser.astype(jnp.bfloat16), embedded, preferred_element_type=jnp.float32)
    first = packed[:, 0:LANES]
    first = jnp.where(empty & (iota(first.shape, 1) == 0), EMPTY, first).astype(jnp.bfloat16)
    rest = packed[:, LANES:].astype(jnp.bfloat16)
    at = 0
    for ref in packed_refs:
        ref[:, 0:LANES] = first[at : at + ref.shape[0]]
        ref[:, LANES:] = rest[at : at + ref.shape[0]]
        at += ref.shape[0]


def order_block(owner, me):
    step = owner ^ me
    block = jnp.zeros_like(step)
    for at, other in enumerate(ORDER, 1):
        block = jnp.where(step == other, at, block)
    return block


def owner_block(owner, _):
    return owner


def embed(me, arrays, sizes, slot_cap, block_of):
    token_states, lengths, cluster_id, proj_weight, proj_bias = arrays
    rows, _, width = token_states.shape
    return pl.pallas_call(
        functools.partial(embed_kernel, slot_cap, block_of),
        out_shape=[jax.ShapeDtypeStruct((size, width), jnp.bfloat16) for size in sizes]
        + [jax.ShapeDtypeStruct((8, rows), jnp.int32)],
        in_specs=[SMEM] + [HBM] * 5,
        out_specs=[VMEM] * (len(sizes) + 1),
        scratch_shapes=[
            pltpu.VMEM(token_states.shape, token_states.dtype),
            pltpu.VMEM(proj_weight.shape, proj_weight.dtype),
            pltpu.VMEM((1, width), jnp.float32),
            pltpu.VMEM((1, rows), jnp.int32),
            pltpu.VMEM((1, rows), jnp.int32),
            pltpu.SemaphoreType.DMA((4 + WEIGHT_PARTS,)),
        ],
        compiler_params=PARAMS,
        name="embed",
    )(
        me,
        in_hbm(token_states),
        in_hbm(lengths.reshape(1, rows)),
        in_hbm(cluster_id.reshape(1, rows)),
        in_hbm(proj_weight),
        in_hbm(proj_bias.reshape(1, width)),
    )


def join_kernel(*refs):
    *in_refs, out_ref = refs
    at = 0
    for ref in in_refs:
        out_ref[pl.ds(at, ref.shape[0]), :] = ref[...]
        at += ref.shape[0]


def join(blocks):
    rows = sum(block.shape[0] for block in blocks)
    return pl.pallas_call(
        join_kernel,
        out_shape=jax.ShapeDtypeStruct((rows, blocks[0].shape[1]), blocks[0].dtype),
        in_specs=[VMEM] * len(blocks),
        out_specs=VMEM,
        compiler_params=PARAMS,
        name="join",
    )(*blocks)


def best_of(scores, rows):
    valid = rows[:, 0:LANES].astype(jnp.float32)[:, 0:1] < 1.5
    return jnp.max(jnp.where(valid, scores, -1.0), axis=0, keepdims=True)


def inner_kernel(mine_ref, best_ref, turned_ref):
    turned = mine_ref[...].T
    turned_ref[...] = turned
    scores = jnp.dot(mine_ref[...], turned, preferred_element_type=jnp.float32)
    itself = iota(scores.shape, 0) == iota(scores.shape, 1)
    best_ref[...] = best_of(jnp.where(itself, -1.0, scores), mine_ref)


def inner_best(mine):
    slots, width = mine.shape
    return pl.pallas_call(
        inner_kernel,
        out_shape=(
            jax.ShapeDtypeStruct((1, slots), jnp.float32),
            jax.ShapeDtypeStruct((width, slots), mine.dtype),
        ),
        in_specs=[VMEM],
        out_specs=(VMEM, VMEM),
        compiler_params=PARAMS,
        name="inner",
    )(mine)


def score_kernel(slot_cap, sources_of, me_ref, best_ref, turned_ref, other_ref, out_ref):
    scores = jnp.dot(other_ref[...], turned_ref[...], preferred_element_type=jnp.float32)
    maxima = jnp.maximum(best_ref[...], best_of(scores, other_ref))
    for at, source in enumerate(sources_of(out_ref.shape[0], me_ref[0])):
        out_ref[source, :, 0:slot_cap] = maxima[:, at * slot_cap : (at + 1) * slot_cap]


def order_sources(owners, me):
    return [me] + [me ^ step for step in ORDER]


def owner_sources(owners, _):
    return range(owners)


def score(me, mine, other, owners, slot_cap, sources_of):
    lanes = -(-slot_cap // LANES) * LANES
    return pl.pallas_call(
        functools.partial(score_kernel, slot_cap, sources_of),
        out_shape=jax.ShapeDtypeStruct((owners, 1, lanes), jnp.float32),
        in_specs=[SMEM] + [VMEM] * 3,
        out_specs=VMEM,
        compiler_params=PARAMS,
        name="score",
    )(me, *inner_best(mine), other)


def pick_kernel(returned_ref, place_ref, out_ref):
    owners, _, lanes = returned_ref.shape
    rows = place_ref.shape[1]
    owner = place_ref[0:1, :]
    rank = jnp.broadcast_to(place_ref[1:2, :], (owners, rows))
    returned = returned_ref[...].reshape(owners, lanes)
    taken = jnp.take_along_axis(returned, rank, axis=1, mode="promise_in_bounds")
    taken = jnp.where(iota((owners, rows), 0) == owner, taken, -3.0)
    out_ref[...] = jnp.max(taken, axis=0, keepdims=True)


def pick(returned, place):
    rows = place.shape[1]
    return pl.pallas_call(
        pick_kernel,
        out_shape=jax.ShapeDtypeStruct((1, rows), jnp.float32),
        in_specs=[VMEM, VMEM],
        out_specs=VMEM,
        name="pick",
    )(in_vmem(returned), in_vmem(place)).reshape(rows)


def rows_of_devices(helpers, docs):
    return [[doc * helpers + (row ^ turn(doc)) for doc in range(docs)] for row in range(helpers)]


def step_to(value, step):
    rows = rows_of_devices(lax.axis_size("help"), lax.axis_size("docs"))
    pairs = [(row[doc], row[doc ^ step]) for row in rows for doc in range(len(row))]
    return lax.ppermute(value, ("docs", "help"), pairs)


def exchange(value):
    rows = rows_of_devices(lax.axis_size("help"), lax.axis_size("docs"))
    return lax.all_to_all(
        value, ("docs", "help"), split_axis=0, concat_axis=0, tiled=True, axis_index_groups=rows
    )


def swap(value):
    return lax.ppermute(value, "help", [(i, i ^ 1) for i in range(lax.axis_size("help"))])


def body(*arrays):
    owners = lax.axis_size("docs")
    slot_cap = 2 * arrays[0].shape[0] // owners
    me = lax.axis_index("docs").reshape(1)
    if owners == len(ORDER) + 1:
        block_of, sources_of = order_block, order_sources
        own, *blocks, place = embed(me, arrays, [slot_cap] * owners, slot_cap, block_of)
        mine = join([own] + [step_to(*send) for send in zip(blocks, ORDER)])
    else:
        block_of, sources_of = owner_block, owner_sources
        packed, place = embed(me, arrays, [owners * slot_cap], slot_cap, block_of)
        mine = exchange(packed)
    maxima = score(me, mine, swap(mine), owners, slot_cap, sources_of)
    returned = exchange(maxima)
    return pick(returned, place)


def solution(mesh):
    spread = P(("groups", "docs", "help"))
    in_specs = (P(("groups", "docs", "help"), None, None), spread, spread, P(), P())
    return jax.shard_map(body, mesh=mesh, in_specs=in_specs, out_specs=spread, check_vma=False)
```

```python
import functools

import jax
import jax.numpy as jnp
from jax import lax
from jax.experimental import pallas as pl
from jax.experimental.pallas import tpu as pltpu
from jax.sharding import PartitionSpec as P

CL_OWN = 1
LANES = 128
EMPTY = 2.0
WEIGHT_PARTS = 4
VMEM = pl.BlockSpec(memory_space=pltpu.VMEM)
SMEM = pl.BlockSpec(memory_space=pltpu.SMEM)
HBM = pl.BlockSpec(memory_space=pltpu.HBM)
PARAMS = pltpu.CompilerParams(vmem_limit_bytes=32 * 2**20)

ORDER = (6, 1, 7, 2, 5, 3, 4)


def turn(doc):
    return (doc >> 2) & 1


def iota(shape, dim):
    return lax.broadcasted_iota(jnp.int32, shape, dim)


def in_hbm(array):
    return pltpu.with_memory_space_constraint(array, pltpu.HBM)


def in_vmem(array):
    return pltpu.with_memory_space_constraint(array, pltpu.VMEM)


def embed_kernel(
    slot_cap, block_of, me_ref,
    tok_hbm, len_hbm, id_hbm, weight_hbm, bias_hbm, *refs,
):
    *packed_refs, place_ref, tok, weight, bias, lens, ids, sems = refs
    rows, seq_len, _ = tok.shape
    slots = sum(ref.shape[0] for ref in packed_refs)
    pairs = [(len_hbm, lens), (id_hbm, ids), (tok_hbm, tok), (bias_hbm, bias)]
    part = weight.shape[0] // WEIGHT_PARTS
    for at in range(WEIGHT_PARTS):
        pairs.append((weight_hbm.at[pl.ds(at * part, part)], weight.at[pl.ds(at * part, part)]))
    copies = [
        pltpu.make_async_copy(source, target, sems.at[at])
        for at, (source, target) in enumerate(pairs)
    ]
    for copy in copies:
        copy.start()
    diagonal = iota((rows, rows), 0) == iota((rows, rows), 1)

    def column(row):
        return jnp.sum(jnp.where(diagonal, row, 0), axis=1, keepdims=True)

    copies[0].wait()
    copies[1].wait()
    counts = column(lens[...])
    owner = ids[...] // CL_OWN
    earlier = (column(owner) == owner) & (iota((rows, rows), 0) < iota((rows, rows), 1))
    rank = jnp.sum(earlier.astype(jnp.int32), axis=0, keepdims=True)
    place_ref[0:1, :] = owner
    place_ref[1:2, :] = rank
    block = block_of(owner, me_ref[0])
    chooser = iota((slots, rows), 0) == block * slot_cap + rank
    chooser = jnp.where(chooser, 1.0, 0.0)
    empty = jnp.sum(chooser, axis=1, keepdims=True) < 0.5
    copies[2].wait()
    summed = tok[:, 0, :].astype(jnp.float32)
    for t in range(1, seq_len):
        summed += jnp.where(counts > t, tok[:, t, :].astype(jnp.float32), 0.0)
    pooled = (summed / counts.astype(jnp.float32)).astype(jnp.bfloat16)
    for copy in copies[3:]:
        copy.wait()
    hidden = jnp.tanh(
        jnp.dot(pooled, weight[...], preferred_element_type=jnp.float32) + bias[...]
    )
    factor = lax.rsqrt(jnp.sum(hidden * hidden, axis=1, keepdims=True) + 1e-06)
    embedded = (hidden * factor).astype(jnp.bfloat16)
    packed = jnp.dot(chooser.astype(jnp.bfloat16), embedded, preferred_element_type=jnp.float32)
    first = packed[:, 0:LANES]
    first = jnp.where(empty & (iota(first.shape, 1) == 0), EMPTY, first).astype(jnp.bfloat16)
    rest = packed[:, LANES:].astype(jnp.bfloat16)
    at = 0
    for ref in packed_refs:
        ref[:, 0:LANES] = first[at : at + ref.shape[0]]
        ref[:, LANES:] = rest[at : at + ref.shape[0]]
        at += ref.shape[0]


def order_block(owner, me):
    step = owner ^ me
    block = jnp.zeros_like(step)
    for at, other in enumerate(ORDER, 1):
        block = jnp.where(step == other, at, block)
    return block


def owner_block(owner, _):
    return owner


def embed(me, arrays, sizes, slot_cap, block_of):
    token_states, lengths, cluster_id, proj_weight, proj_bias = arrays
    rows, _, width = token_states.shape
    return pl.pallas_call(
        functools.partial(embed_kernel, slot_cap, block_of),
        out_shape=[jax.ShapeDtypeStruct((size, width), jnp.bfloat16) for size in sizes]
        + [jax.ShapeDtypeStruct((8, rows), jnp.int32)],
        in_specs=[SMEM] + [HBM] * 5,
        out_specs=[VMEM] * (len(sizes) + 1),
        scratch_shapes=[
            pltpu.VMEM(token_states.shape, token_states.dtype),
            pltpu.VMEM(proj_weight.shape, proj_weight.dtype),
            pltpu.VMEM((1, width), jnp.float32),
            pltpu.VMEM((1, rows), jnp.int32),
            pltpu.VMEM((1, rows), jnp.int32),
            pltpu.SemaphoreType.DMA((4 + WEIGHT_PARTS,)),
        ],
        compiler_params=PARAMS,
        name="embed",
    )(
        me,
        in_hbm(token_states),
        in_hbm(lengths.reshape(1, rows)),
        in_hbm(cluster_id.reshape(1, rows)),
        in_hbm(proj_weight),
        in_hbm(proj_bias.reshape(1, width)),
    )


def join_kernel(*refs):
    *in_refs, out_ref = refs
    at = 0
    for ref in in_refs:
        out_ref[pl.ds(at, ref.shape[0]), :] = ref[...]
        at += ref.shape[0]


def join(blocks):
    rows = sum(block.shape[0] for block in blocks)
    return pl.pallas_call(
        join_kernel,
        out_shape=jax.ShapeDtypeStruct((rows, blocks[0].shape[1]), blocks[0].dtype),
        in_specs=[VMEM] * len(blocks),
        out_specs=VMEM,
        compiler_params=PARAMS,
        name="join",
    )(*blocks)


def best_of(scores, rows):
    valid = rows[:, 0:LANES].astype(jnp.float32)[:, 0:1] < 1.5
    return jnp.max(jnp.where(valid, scores, -1.0), axis=0, keepdims=True)


def inner_kernel(mine_ref, best_ref, turned_ref):
    turned = mine_ref[...].T
    turned_ref[...] = turned
    scores = jnp.dot(mine_ref[...], turned, preferred_element_type=jnp.float32)
    itself = iota(scores.shape, 0) == iota(scores.shape, 1)
    best_ref[...] = best_of(jnp.where(itself, -1.0, scores), mine_ref)


def inner_best(mine):
    slots, width = mine.shape
    return pl.pallas_call(
        inner_kernel,
        out_shape=(
            jax.ShapeDtypeStruct((1, slots), jnp.float32),
            jax.ShapeDtypeStruct((width, slots), mine.dtype),
        ),
        in_specs=[VMEM],
        out_specs=(VMEM, VMEM),
        compiler_params=PARAMS,
        name="inner",
    )(mine)


def score_kernel(slot_cap, sources_of, me_ref, best_ref, turned_ref, other_ref, out_ref):
    scores = jnp.dot(other_ref[...], turned_ref[...], preferred_element_type=jnp.float32)
    maxima = jnp.maximum(best_ref[...], best_of(scores, other_ref))
    for at, source in enumerate(sources_of(out_ref.shape[0], me_ref[0])):
        out_ref[source, :, 0:slot_cap] = maxima[:, at * slot_cap : (at + 1) * slot_cap]


def order_sources(owners, me):
    return [me] + [me ^ step for step in ORDER]


def owner_sources(owners, _):
    return range(owners)


def score(me, mine, other, owners, slot_cap, sources_of):
    lanes = -(-slot_cap // LANES) * LANES
    return pl.pallas_call(
        functools.partial(score_kernel, slot_cap, sources_of),
        out_shape=jax.ShapeDtypeStruct((owners, 1, lanes), jnp.float32),
        in_specs=[SMEM] + [VMEM] * 3,
        out_specs=VMEM,
        compiler_params=PARAMS,
        name="score",
    )(me, *inner_best(mine), other)


def pick_kernel(returned_ref, place_ref, out_ref):
    owners, _, lanes = returned_ref.shape
    rows = place_ref.shape[1]
    owner = place_ref[0:1, :]
    rank = jnp.broadcast_to(place_ref[1:2, :], (owners, rows))
    returned = returned_ref[...].reshape(owners, lanes)
    taken = jnp.take_along_axis(returned, rank, axis=1, mode="promise_in_bounds")
    taken = jnp.where(iota((owners, rows), 0) == owner, taken, -3.0)
    out_ref[...] = jnp.max(taken, axis=0, keepdims=True)


def pick(returned, place):
    rows = place.shape[1]
    return pl.pallas_call(
        pick_kernel,
        out_shape=jax.ShapeDtypeStruct((1, rows), jnp.float32),
        in_specs=[VMEM, VMEM],
        out_specs=VMEM,
        name="pick",
    )(in_vmem(returned), in_vmem(place)).reshape(rows)


def rows_of_devices(helpers, docs):
    return [[doc * helpers + (row ^ turn(doc)) for doc in range(docs)] for row in range(helpers)]


def step_to(value, step):
    rows = rows_of_devices(lax.axis_size("help"), lax.axis_size("docs"))
    pairs = [(row[doc], row[doc ^ step]) for row in rows for doc in range(len(row))]
    return lax.ppermute(value, ("docs", "help"), pairs)


def exchange(value):
    rows = rows_of_devices(lax.axis_size("help"), lax.axis_size("docs"))
    return lax.all_to_all(
        value, ("docs", "help"), split_axis=0, concat_axis=0, tiled=True, axis_index_groups=rows
    )


def swap(value):
    return lax.ppermute(value, "help", [(i, i ^ 1) for i in range(lax.axis_size("help"))])


def body(*arrays):
    owners = lax.axis_size("docs")
    slot_cap = 2 * arrays[0].shape[0] // owners
    me = lax.axis_index("docs").reshape(1)
    if owners == len(ORDER) + 1:
        block_of, sources_of = order_block, order_sources
        own, *blocks, place = embed(me, arrays, [slot_cap] * owners, slot_cap, block_of)
        mine = join([own] + [step_to(*send) for send in zip(blocks, ORDER)])
    else:
        block_of, sources_of = owner_block, owner_sources
        packed, place = embed(me, arrays, [owners * slot_cap], slot_cap, block_of)
        mine = exchange(packed)
    maxima = score(me, mine, swap(mine), owners, slot_cap, sources_of)
    returned = exchange(maxima)
    return pick(returned, place)


def solution(mesh):
    spread = P(("groups", "docs", "help"))
    in_specs = (P(("groups", "docs", "help"), None, None), spread, spread, P(), P())
    return jax.shard_map(body, mesh=mesh, in_specs=in_specs, out_specs=spread, check_vma=False)
```

```python
import functools

import jax
import jax.numpy as jnp
from jax import lax
from jax.experimental import pallas as pl
from jax.experimental.pallas import tpu as pltpu
from jax.sharding import PartitionSpec as P

CL_OWN = 1
LANES = 128
EMPTY = 2.0
WEIGHT_PARTS = 4
VMEM = pl.BlockSpec(memory_space=pltpu.VMEM)
SMEM = pl.BlockSpec(memory_space=pltpu.SMEM)
HBM = pl.BlockSpec(memory_space=pltpu.HBM)
PARAMS = pltpu.CompilerParams(vmem_limit_bytes=32 * 2**20)

ORDER = (6, 1, 7, 2, 5, 3, 4)


def turn(doc):
    return (doc >> 2) & 1


def iota(shape, dim):
    return lax.broadcasted_iota(jnp.int32, shape, dim)


def in_hbm(array):
    return pltpu.with_memory_space_constraint(array, pltpu.HBM)


def in_vmem(array):
    return pltpu.with_memory_space_constraint(array, pltpu.VMEM)


def embed_kernel(
    slot_cap, block_of, me_ref,
    tok_hbm, len_hbm, id_hbm, weight_hbm, bias_hbm, *refs,
):
    *packed_refs, place_ref, tok, weight, bias, lens, ids, sems = refs
    rows, seq_len, _ = tok.shape
    slots = sum(ref.shape[0] for ref in packed_refs)
    pairs = [(len_hbm, lens), (id_hbm, ids), (tok_hbm, tok), (bias_hbm, bias)]
    part = weight.shape[0] // WEIGHT_PARTS
    for at in range(WEIGHT_PARTS):
        pairs.append((weight_hbm.at[pl.ds(at * part, part)], weight.at[pl.ds(at * part, part)]))
    copies = [
        pltpu.make_async_copy(source, target, sems.at[at])
        for at, (source, target) in enumerate(pairs)
    ]
    for copy in copies:
        copy.start()
    diagonal = iota((rows, rows), 0) == iota((rows, rows), 1)

    def column(row):
        return jnp.sum(jnp.where(diagonal, row, 0), axis=1, keepdims=True)

    copies[0].wait()
    copies[1].wait()
    counts = column(lens[...])
    owner = ids[...] // CL_OWN
    earlier = (column(owner) == owner) & (iota((rows, rows), 0) < iota((rows, rows), 1))
    rank = jnp.sum(earlier.astype(jnp.int32), axis=0, keepdims=True)
    place_ref[0:1, :] = owner
    block, spot = block_of(owner, me_ref[0])
    place_ref[2:3, :] = spot * slot_cap + rank
    chooser = iota((slots, rows), 0) == block * slot_cap + rank
    chooser = jnp.where(chooser, 1.0, 0.0)
    empty = jnp.sum(chooser, axis=1, keepdims=True) < 0.5
    copies[2].wait()
    summed = tok[:, 0, :].astype(jnp.float32)
    for t in range(1, seq_len):
        summed += jnp.where(counts > t, tok[:, t, :].astype(jnp.float32), 0.0)
    pooled = (summed / counts.astype(jnp.float32)).astype(jnp.bfloat16)
    for copy in copies[3:]:
        copy.wait()
    hidden = jnp.tanh(
        jnp.dot(pooled, weight[...], preferred_element_type=jnp.float32) + bias[...]
    )
    factor = lax.rsqrt(jnp.sum(hidden * hidden, axis=1, keepdims=True) + 1e-06)
    embedded = (hidden * factor).astype(jnp.bfloat16)
    packed = jnp.dot(chooser.astype(jnp.bfloat16), embedded, preferred_element_type=jnp.float32)
    first = packed[:, 0:LANES]
    first = jnp.where(empty & (iota(first.shape, 1) == 0), EMPTY, first).astype(jnp.bfloat16)
    rest = packed[:, LANES:].astype(jnp.bfloat16)
    at = 0
    for ref in packed_refs:
        ref[:, 0:LANES] = first[at : at + ref.shape[0]]
        ref[:, LANES:] = rest[at : at + ref.shape[0]]
        at += ref.shape[0]


def order_block(owner, me):
    step = owner ^ me
    block = jnp.zeros_like(step)
    for at, other in enumerate(ORDER, 1):
        block = jnp.where(step == other, at, block)
    return block, block


def owner_block(owner, me):
    return owner, me


def embed(me, arrays, sizes, slot_cap, block_of):
    token_states, lengths, cluster_id, proj_weight, proj_bias = arrays
    rows, _, width = token_states.shape
    return pl.pallas_call(
        functools.partial(embed_kernel, slot_cap, block_of),
        out_shape=[jax.ShapeDtypeStruct((size, width), jnp.bfloat16) for size in sizes]
        + [jax.ShapeDtypeStruct((8, rows), jnp.int32)],
        in_specs=[SMEM] + [HBM] * 5,
        out_specs=[VMEM] * (len(sizes) + 1),
        scratch_shapes=[
            pltpu.VMEM(token_states.shape, token_states.dtype),
            pltpu.VMEM(proj_weight.shape, proj_weight.dtype),
            pltpu.VMEM((1, width), jnp.float32),
            pltpu.VMEM((1, rows), jnp.int32),
            pltpu.VMEM((1, rows), jnp.int32),
            pltpu.SemaphoreType.DMA((4 + WEIGHT_PARTS,)),
        ],
        compiler_params=PARAMS,
        name="embed",
    )(
        me,
        in_hbm(token_states),
        in_hbm(lengths.reshape(1, rows)),
        in_hbm(cluster_id.reshape(1, rows)),
        in_hbm(proj_weight),
        in_hbm(proj_bias.reshape(1, width)),
    )


def join_kernel(*refs):
    *in_refs, out_ref = refs
    at = 0
    for ref in in_refs:
        out_ref[pl.ds(at, ref.shape[0]), :] = ref[...]
        at += ref.shape[0]


def join(blocks):
    rows = sum(block.shape[0] for block in blocks)
    return pl.pallas_call(
        join_kernel,
        out_shape=jax.ShapeDtypeStruct((rows, blocks[0].shape[1]), blocks[0].dtype),
        in_specs=[VMEM] * len(blocks),
        out_specs=VMEM,
        compiler_params=PARAMS,
        name="join",
    )(*blocks)


def best_of(scores, rows):
    valid = rows[:, 0:LANES].astype(jnp.float32)[:, 0:1] < 1.5
    return jnp.max(jnp.where(valid, scores, -1.0), axis=0, keepdims=True)


def inner_kernel(mine_ref, best_ref, turned_ref):
    turned = mine_ref[...].T
    turned_ref[...] = turned
    scores = jnp.dot(mine_ref[...], turned, preferred_element_type=jnp.float32)
    itself = iota(scores.shape, 0) == iota(scores.shape, 1)
    best_ref[...] = best_of(jnp.where(itself, -1.0, scores), mine_ref)


def inner_best(mine):
    slots, width = mine.shape
    return pl.pallas_call(
        inner_kernel,
        out_shape=(
            jax.ShapeDtypeStruct((1, slots), jnp.float32),
            jax.ShapeDtypeStruct((width, slots), mine.dtype),
        ),
        in_specs=[VMEM],
        out_specs=(VMEM, VMEM),
        compiler_params=PARAMS,
        name="inner",
    )(mine)


def score_kernel(best_ref, turned_ref, other_ref, out_ref):
    scores = jnp.dot(other_ref[...], turned_ref[...], preferred_element_type=jnp.float32)
    maxima = jnp.maximum(best_ref[...], best_of(scores, other_ref))
    for source in range(out_ref.shape[0]):
        out_ref[source] = maxima


def score(mine, other, owners):
    return pl.pallas_call(
        score_kernel,
        out_shape=jax.ShapeDtypeStruct((owners, 1, mine.shape[0]), jnp.float32),
        in_specs=[VMEM] * 3,
        out_specs=VMEM,
        compiler_params=PARAMS,
        name="score",
    )(*inner_best(mine), other)


def pick_kernel(returned_ref, place_ref, out_ref):
    owners, _, lanes = returned_ref.shape
    rows = place_ref.shape[1]
    owner = place_ref[0:1, :]
    slot = jnp.broadcast_to(place_ref[2:3, :], (owners, rows))
    returned = returned_ref[...].reshape(owners, lanes)
    taken = jnp.full((owners, rows), -3.0)
    for start in range(0, lanes, rows):
        part = slot - start
        inside = (part >= 0) & (part < rows)
        part = jnp.where(inside, part, 0)
        found = jnp.take_along_axis(
            returned[:, start : start + rows], part, axis=1, mode="promise_in_bounds"
        )
        taken = jnp.where(inside, found, taken)
    taken = jnp.where(iota((owners, rows), 0) == owner, taken, -3.0)
    out_ref[...] = jnp.max(taken, axis=0, keepdims=True)


def pick(returned, place):
    rows = place.shape[1]
    return pl.pallas_call(
        pick_kernel,
        out_shape=jax.ShapeDtypeStruct((1, rows), jnp.float32),
        in_specs=[VMEM, VMEM],
        out_specs=VMEM,
        name="pick",
    )(in_vmem(returned), in_vmem(place)).reshape(rows)


def rows_of_devices(helpers, docs):
    return [[doc * helpers + (row ^ turn(doc)) for doc in range(docs)] for row in range(helpers)]


def step_to(value, step):
    rows = rows_of_devices(lax.axis_size("help"), lax.axis_size("docs"))
    pairs = [(row[doc], row[doc ^ step]) for row in rows for doc in range(len(row))]
    return lax.ppermute(value, ("docs", "help"), pairs)


def exchange(value):
    rows = rows_of_devices(lax.axis_size("help"), lax.axis_size("docs"))
    return lax.all_to_all(
        value, ("docs", "help"), split_axis=0, concat_axis=0, tiled=True, axis_index_groups=rows
    )


def swap(value):
    return lax.ppermute(value, "help", [(i, i ^ 1) for i in range(lax.axis_size("help"))])


def body(*arrays):
    owners = lax.axis_size("docs")
    slot_cap = 2 * arrays[0].shape[0] // owners
    me = lax.axis_index("docs").reshape(1)
    if owners == len(ORDER) + 1:
        block_of = order_block
        own, *blocks, place = embed(me, arrays, [slot_cap] * owners, slot_cap, block_of)
        mine = join([own] + [step_to(*send) for send in zip(blocks, ORDER)])
    else:
        block_of = owner_block
        packed, place = embed(me, arrays, [owners * slot_cap], slot_cap, block_of)
        mine = exchange(packed)
    maxima = score(mine, swap(mine), owners)
    returned = exchange(maxima)
    return pick(returned, place)


def solution(mesh):
    spread = P(("groups", "docs", "help"))
    in_specs = (P(("groups", "docs", "help"), None, None), spread, spread, P(), P())
    return jax.shard_map(body, mesh=mesh, in_specs=in_specs, out_specs=spread, check_vma=False)
```
